32 devices in a mesh: groups: 2 (over y), sector: 4 (over z), op: 2 (over x), sub: 2 (over core).
Axes of the slice: x: 2, y: 2, z: 4, core: 2. Of those that a mesh axis runs over, the one named last changes fastest.
Arguments:
- wavefunction: bfloat16 [8, 4, 2, 128, 128], P(('groups', 'sector')), parts along dimension 0, may hold values from -6 to 6
- right_env: bfloat16 [32, 4, 128, 128], P(('groups', 'op', 'sub'), 'sector'), parts along dimension 0, may hold values from -0.5 to 0.5
- left_env: bfloat16 [32, 4, 128, 128], P(('groups', 'op', 'sub'), 'sector'), parts along dimension 0, may hold values from -0.5 to 0.5
- site_ops: float32 [32, 2, 2], P(('groups', 'op', 'sub')), parts along dimension 0, may hold values from -1 to 1
- right_map: int32 [32, 4], P(('groups', 'op', 'sub')), parts along dimension 0, may hold values from 0 to 3
- left_map: int32 [32, 4], P(('groups', 'op', 'sub')), parts along dimension 0, may hold values from 0 to 3
Outputs:
- sigma: bfloat16 [8, 4, 2, 128, 128], P(('groups', 'op', 'sub'), 'sector'), parts along dimension 0
The draws below stay inside these ranges and needn't reach their ends.
There are 2 independent parts, one for each index of `groups`. The reference program is written for one: setup_inputs(seed, part) draws one part's arguments, and reference() takes and returns one part's arrays. A program takes and returns all parts, laid end to end along the dimension named above; each array names one. Nothing has to cross between parts.
All inputs are finite; a program needn't handle non-finite values.
Results may differ from the reference program's by a relative error of at most 0.0058.
Values may be sent and summed in bfloat16 or wider, within the bound.
A program may use at most 64 MiB of HBM per device.

```python
import jax
import jax.numpy as jnp
from jax import lax

BLOCK = 128
CHANNELS = 2
SECTORS = 4
TERMS = 16


def plant(drawn, stream_key, low, high):
    dims = drawn.shape
    index_at = [jax.random.randint(jax.random.fold_in(stream_key, axis), (), 0, dims[axis]) for axis in range(len(dims))]
    drawn = drawn.at[tuple(index_at)].set(low)
    longest = dims.index(max(dims))
    index_at[longest] = (index_at[longest] + 1) % dims[longest]
    return drawn.at[tuple(index_at)].set(high)


def shard_levels(own_key, extent, shards, low, top_value):
    gain = 1.0
    for dim, blocks in shards:
        draws = jax.random.uniform(jax.random.fold_in(jax.random.fold_in(own_key, 6), dim), (blocks,), jnp.float32, low / len(shards), top_value / len(shards))
        gain = gain * jnp.repeat(jnp.exp(draws), extent[dim] // blocks).reshape((-1,) + (1,) * (len(extent) - 1 - dim))
    return gain


def bell_draw(own_key, extent, scale, reach, cuts=(), kind=jnp.bfloat16):
    result = jax.random.normal(own_key, extent, jnp.float32) * scale
    if len(cuts) > 0:
        result = shard_levels(own_key, extent, cuts, -0.22, 0.18) * result
    return jnp.clip(result, min=-reach, max=reach).astype(kind)


def setup_inputs(seed: int = 0, part: int = 0) -> dict:
    key_list = jax.random.split(jax.random.key(seed), 7)
    part_keys = jax.random.split(jax.random.fold_in(key_list[6], part), 7)
    return {
        "wavefunction": bell_draw(part_keys[0], (SECTORS, SECTORS, CHANNELS, BLOCK, BLOCK), 1.0, 6.0, ((0, 4),)),
        "right_env": bell_draw(part_keys[1], (TERMS, SECTORS, BLOCK, BLOCK), BLOCK ** -0.5, 0.5, ((0, 4), (1, 4))),
        "left_env": bell_draw(part_keys[2], (TERMS, SECTORS, BLOCK, BLOCK), BLOCK ** -0.5, 0.5, ((0, 4), (1, 4))),
        "site_ops": bell_draw(part_keys[3], (TERMS, CHANNELS, CHANNELS), (CHANNELS * TERMS) ** -0.5, 1.0, ((0, 4),), jnp.float32),
        "right_map": plant(jax.random.randint(part_keys[4], (TERMS, SECTORS), 0, SECTORS), jax.random.fold_in(part_keys[4], 1), 0, SECTORS - 1).astype(jnp.int32),
        "left_map": plant(jax.random.randint(part_keys[5], (TERMS, SECTORS), 0, SECTORS), jax.random.fold_in(part_keys[5], 1), 0, SECTORS - 1).astype(jnp.int32),
    }


def reference(wavefunction, right_env, left_env, site_ops, right_map, left_map):
    highest = lax.Precision.HIGHEST
    sector_ids = jnp.arange(SECTORS, dtype=jnp.int32)
    wave_float = wavefunction.astype(jnp.float32)

    def one_term(accumulated, inputs):
        right_block, left_block, site_block, right_row, left_row = inputs
        images = jnp.einsum('abpij,bjl->abpil', wave_float, right_block.astype(jnp.float32), precision=highest)
        select = (right_row[:, None] == sector_ids[None, :]).astype(jnp.float32)
        routed = jnp.einsum('bc,abpil->acpil', select, images, precision=highest)
        coupled = jnp.einsum('pq,acpil->acqil', site_block.astype(jnp.float32), routed, precision=highest).astype(jnp.bfloat16)
        products = jnp.einsum('aim,acqil->acqml', left_block.astype(jnp.float32), coupled.astype(jnp.float32), precision=highest).astype(jnp.bfloat16)
        source = (left_row[:, None] == sector_ids[None, :]).astype(jnp.float32)
        accumulated = accumulated + jnp.einsum('ad,acqml->dcqml', source, products.astype(jnp.float32), precision=highest)
        return accumulated, None

    initial = jnp.zeros((SECTORS, SECTORS, CHANNELS, BLOCK, BLOCK), jnp.float32)
    accumulated, unused = lax.scan(one_term, initial, (right_env, left_env, site_ops, right_map, left_map))
    return accumulated.astype(jnp.bfloat16)
```

```python
import functools

import jax
import jax.numpy as jnp
from jax import lax
from jax.experimental import pallas as pl
from jax.experimental.pallas import tpu as pltpu
from jax.sharding import PartitionSpec as P

MESH = pl.DeviceIdType.MESH
BF16 = jnp.bfloat16
F32 = jnp.float32
PARTS = 1


def routed_plan(wavefunction, right_env, left_env, site_ops, right_map, left_map):
    highest = lax.Precision.HIGHEST
    term_count = right_env.shape[0]
    sectors = wavefunction.shape[1]
    sector_ids = jnp.arange(sectors, dtype=jnp.int32)
    right_full = lax.all_gather(right_env, "sector", axis=1, tiled=True)
    coupled_terms = []
    for term_index in range(term_count):
        images = jnp.einsum(
            "abpij,bjl->bapil",
            wavefunction,
            right_full[term_index],
            preferred_element_type=jnp.float32,
        )
        select = (right_map[term_index][:, None] == sector_ids[None, :]).astype(jnp.float32)
        routed = jnp.einsum("bc,bapil->acpil", select, images, precision=highest)
        coupled = jnp.einsum(
            "pq,acpil->acqil", site_ops[term_index], routed, precision=highest
        ).astype(jnp.bfloat16)
        coupled_terms.append(coupled)
    coupled_all = jnp.stack(coupled_terms, axis=0)
    source_select = (left_map[:, :, None] == sector_ids[None, None, :]).astype(jnp.bfloat16)
    local_products = jnp.einsum(
        "taim,tacqil->tacqml", left_env, coupled_all, preferred_element_type=jnp.float32
    ).astype(jnp.bfloat16)
    term_partial = jnp.einsum(
        "tad,tacqml->dcqml",
        source_select,
        lax.all_to_all(local_products, "sector", split_axis=2, concat_axis=1, tiled=True),
        preferred_element_type=jnp.float32,
    )
    reduced = lax.psum_scatter(term_partial, ("op", "sub"), scatter_dimension=0, tiled=True)
    return reduced.astype(jnp.bfloat16)


def fused_kernel(Z, O, U, K, D, Q, N, H, order, psi_ref, r_ref, l_ref, tab_ref, out_ref, stage, rbuf, lbuf, tabs, lm, mask, cp, pf, psend, prcv, fin,
                 t_send, t_recv, up_send, dn_send, l_send, l_recv, tab_send, tab_recv, p_send, p_recv, f_send, f_recv):
    T = O * U
    W = N // T
    LH = W // H
    z = lax.axis_index("sector")
    o = lax.axis_index("op")
    u = lax.axis_index("sub")
    t = o * U + u
    peers = []
    for i in range(O):
        for j in range(U):
            if i or j:
                po, pu = lax.rem(o + i, O), lax.rem(u + j, U)
                peers.append((i * U + j, po * U + pu, {"op": po, "sub": pu}))
    zpeers = [(r, lax.rem(z + r, Z)) for r in range(1, Z)]

    barrier = pltpu.get_barrier_semaphore()
    for e, pt, dev in peers:
        pl.semaphore_signal(barrier, inc=1, device_id=dev, device_id_type=MESH)
    for r, pz in zpeers:
        pl.semaphore_signal(barrier, inc=1, device_id={"sector": pz}, device_id_type=MESH)

    for k in range(K):
        turned = r_ref[k, 0].astype(F32).T.astype(BF16)
        for tt in range(T):
            for h in range(H):
                at = tt * W + h * LH
                stage[tt, h, k] = turned[at:at + LH]
    for h in range(H):
        rbuf[z, h, 0] = stage[t, h]

    pl.semaphore_wait(barrier, len(peers) + len(zpeers))

    def rcopy(e, pt, dev, h):
        return pltpu.make_async_remote_copy(
            src_ref=stage.at[pt, h], dst_ref=rbuf.at[z, h, e],
            send_sem=t_send.at[h, e], recv_sem=t_recv.at[z, h, e], device_id=dev, device_id_type=MESH)

    def tcopy(e, pt, dev):
        return pltpu.make_async_remote_copy(
            src_ref=tab_ref, dst_ref=tabs.at[e - 1],
            send_sem=tab_send.at[e - 1], recv_sem=tab_recv.at[e - 1], device_id=dev, device_id_type=MESH)

    def lcopy(e, pt, dev):
        return pltpu.make_async_remote_copy(
            src_ref=l_ref, dst_ref=lbuf.at[e - 1],
            send_sem=l_send.at[e - 1], recv_sem=l_recv.at[e - 1], device_id=dev, device_id_type=MESH)

    def up(b, h, e):
        return pltpu.make_async_remote_copy(
            src_ref=rbuf.at[b, h, e], dst_ref=rbuf.at[b, h, e],
            send_sem=up_send.at[b, h, e], recv_sem=t_recv.at[b, h, e], device_id={"sector": z + 1}, device_id_type=MESH)

    def down(b, h, e):
        return pltpu.make_async_remote_copy(
            src_ref=rbuf.at[b, h, e], dst_ref=rbuf.at[b, h, e],
            send_sem=dn_send.at[b, h, e], recv_sem=t_recv.at[b, h, e], device_id={"sector": z - 1}, device_id_type=MESH)

    def pcopy(h, r, pz):
        return pltpu.make_async_remote_copy(
            src_ref=psend.at[h, pz], dst_ref=prcv.at[h, z],
            send_sem=p_send.at[h, r - 1], recv_sem=p_recv.at[h, z], device_id={"sector": pz}, device_id_type=MESH)

    def fcopy(h, e, pt, dev):
        return pltpu.make_async_remote_copy(
            src_ref=fin.at[h, pt], dst_ref=out_ref.at[t, h],
            send_sem=f_send.at[h, e - 1], recv_sem=f_recv.at[h, e - 1], device_id=dev, device_id_type=MESH)

    for h in range(H):
        for e, pt, dev in peers:
            rcopy(e, pt, dev, h).start()
        if h == 0:
            for e, pt, dev in peers:
                tcopy(e, pt, dev).start()
    for e, pt, dev in peers:
        lcopy(e, pt, dev).start()

    def gather(h, r):
        if r == 0:
            for e in range(T):
                if e:
                    up(z, h, e).wait_recv()

                @pl.when(z < Z - 1)
                def _():
                    up(z, h, e).start()

                @pl.when(z > 0)
                def _():
                    down(z, h, e).start()
            return
        for e in range(T):
            @pl.when(z - r >= 0)
            def _():
                up(z - r, h, e).wait_recv()

                @pl.when(z < Z - 1)
                def _():
                    up(z - r, h, e).start()

            @pl.when(z + r <= Z - 1)
            def _():
                down(z + r, h, e).wait_recv()

                @pl.when(z > 0)
                def _():
                    down(z + r, h, e).start()

    def table(e):
        return tab_ref[...] if e == 0 else tabs[e - 1]

    def row(tab, at):
        return jnp.broadcast_to(tab[:, at:at + 1], (tab.shape[0], N))

    def prepare():
        for e, pt, dev in peers:
            tcopy(e, pt, dev).wait_recv()
        for e in range(T):
            tab = table(e)
            for b in range(D):
                want = row(tab, b)
                for c in range(D):
                    hit = jnp.where(want == float(c), 1.0, 0.0)
                    for k in range(K):
                        mask[c, (e * K + k) * LH:(e * K + k + 1) * LH, b * N:(b + 1) * N] = jnp.broadcast_to(hit[k:k + 1], (LH, N)).astype(BF16)

    def prepare_left():
        for e, pt, dev in peers:
            lcopy(e, pt, dev).wait_recv()
        for e in range(T):
            want = row(table(e), D)
            for d in range(D):
                hit = jnp.where(want == float(d), 1.0, 0.0)
                for k in range(K):
                    block = l_ref[k, 0] if e == 0 else lbuf[e - 1, k, 0]
                    lm[(e * K + k) * N:(e * K + k + 1) * N, d * N:(d + 1) * N] = block * jnp.broadcast_to(hit[k:k + 1], (N, N)).astype(BF16)

    def compute(h):
        rows = T * K * LH
        right = jnp.concatenate([rbuf[b, h].reshape(rows, N) for b in range(D)], axis=1)
        for c in range(D):
            masked = right * mask[c]
            routed = None
            for b in range(D):
                part = lax.dot_general(masked[:, b * N:(b + 1) * N], psi_ref[0, b].reshape(Q * N, N),
                                       (((1,), (1,)), ((), ())), preferred_element_type=F32)
                routed = part if routed is None else routed + part
            for e in range(T):
                tab = table(e)
                for k in range(K):
                    at = (e * K + k) * LH
                    for q in range(Q):
                        coupled = None
                        for p in range(Q):
                            weight = row(tab, D + 1 + p * Q + q)[k:k + 1]
                            part = routed[at:at + LH, p * N:(p + 1) * N] * weight
                            coupled = part if coupled is None else coupled + part
                        cp[(c * Q + q) * LH:(c * Q + q + 1) * LH, (e * K + k) * N:(e * K + k + 1) * N] = coupled.astype(BF16)

    def products(h):
        sums = jnp.dot(cp[...], lm[...], preferred_element_type=F32)
        for c in range(D):
            part = sums[c * Q * LH:(c + 1) * Q * LH]
            pf[h, c] = part
            psend[h, c] = part.astype(BF16)
        for r, pz in zpeers[::-1]:
            pcopy(h, r, pz).start()

    def finish(h):
        total = pf[h, z]
        for r, pz in zpeers:
            pltpu.make_async_remote_copy(
                src_ref=psend.at[h, pz], dst_ref=prcv.at[h, pz], send_sem=p_send.at[h, r - 1],
                recv_sem=p_recv.at[h, pz], device_id={"sector": pz}, device_id_type=MESH).wait_recv()
            total = total + prcv[h, pz].astype(F32)
        total = total.astype(BF16)
        for d in range(D):
            fin[h, d] = total[:, d * N:(d + 1) * N].reshape(Q, LH, N)
        for e, pt, dev in peers:
            fcopy(h, e, pt, dev).start()
        out_ref[t, h] = fin[h, t]

    for step in order:
        kind = step[0]
        if kind == "gather":
            gather(step[1], step[2])
        elif kind == "prepare":
            prepare()
        elif kind == "left":
            prepare_left()
        elif kind == "compute":
            compute(step[1])
        elif kind == "products":
            products(step[1])
        else:
            finish(step[1])

    for h in range(H):
        for e, pt, dev in peers:
            fcopy(h, e, pt, dev).wait_recv()
            fcopy(h, e, pt, dev).wait_send()
            rcopy(e, pt, dev, h).wait_send()
        for r, pz in zpeers:
            pcopy(h, r, pz).wait_send()
        for e in range(T):
            for r in range(Z):
                @pl.when(jnp.logical_and(z - r >= 0, z < Z - 1))
                def _():
                    up(z - r, h, e).wait_send()

                @pl.when(jnp.logical_and(z + r <= Z - 1, z > 0))
                def _():
                    down(z + r, h, e).wait_send()
    for e, pt, dev in peers:
        tcopy(e, pt, dev).wait_send()
        lcopy(e, pt, dev).wait_send()


def steps(Z, H):
    if H == 1:
        order = [("gather", 0, 0), ("prepare",)]
        order += [("gather", 0, r) for r in range(1, Z - 1)]
        order += [("left",), ("gather", 0, Z - 1), ("compute", 0), ("products", 0), ("finish", 0)]
        return order
    order = [("gather", 0, 0), ("prepare",), ("gather", 0, 1), ("gather", 0, 2), ("gather", 1, 0), ("left",)]
    order += [("gather", 0, 3), ("gather", 1, 1), ("compute", 0), ("products", 0), ("gather", 1, 2)]
    order += [("gather", 1, 3), ("compute", 1), ("products", 1), ("finish", 0), ("finish", 1)]
    return order


def fused_plan(Z, O, U, wavefunction, right_env, left_env, site_ops, right_map, left_map):
    K = right_env.shape[0]
    _, D, Q, N, _ = wavefunction.shape
    T, H = O * U, PARTS
    LH = N // T // H
    own = lax.axis_index("sector")
    left = lax.dynamic_slice_in_dim(left_map, own, 1, axis=1)
    tab = jnp.concatenate([right_map.astype(F32), left.astype(F32), site_ops.reshape(K, Q * Q)], axis=1)
    tab = jnp.pad(tab, ((0, -K % 8), (0, 128 - tab.shape[1])))
    dma = pltpu.SemaphoreType.DMA
    vmem = pl.BlockSpec(memory_space=pltpu.VMEM)
    out = pl.pallas_call(
        functools.partial(fused_kernel, Z, O, U, K, D, Q, N, H, steps(Z, H)),
        out_shape=jax.ShapeDtypeStruct((T, H, Q, LH, N), BF16),
        in_specs=[vmem] * 4,
        out_specs=vmem,
        scratch_shapes=[
            pltpu.VMEM((T, H, K, LH, N), BF16),
            pltpu.VMEM((D, H, T, K, LH, N), BF16),
            pltpu.VMEM((T - 1,) + left_env.shape, BF16),
            pltpu.VMEM((T - 1,) + tab.shape, F32),
            pltpu.VMEM((T * K * N, D * N), BF16),
            pltpu.VMEM((D, T * K * LH, D * N), BF16),
            pltpu.VMEM((D * Q * LH, T * K * N), BF16),
            pltpu.VMEM((H, D, Q * LH, D * N), F32),
            pltpu.VMEM((H, D, Q * LH, D * N), BF16),
            pltpu.VMEM((H, D, Q * LH, D * N), BF16),
            pltpu.VMEM((H, D, Q, LH, N), BF16),
            dma((H, T)), dma((D, H, T)), dma((D, H, T)), dma((D, H, T)),
            dma((T - 1,)), dma((T - 1,)), dma((T - 1,)), dma((T - 1,)),
            dma((H, Z - 1)), dma((H, Z)), dma((H, T - 1)), dma((H, T - 1)),
        ],
        compiler_params=pltpu.CompilerParams(collective_id=0, has_side_effects=True, vmem_limit_bytes=40 << 20),
        name="sigma",
    )(wavefunction, right_env, left_env, tab)
    out = out.transpose(2, 4, 0, 1, 3).reshape(1, 1, Q, N, N)
    return out


def solution(mesh):
    shape = mesh.shape
    Z, O, U = shape["sector"], shape["op"], shape["sub"]

    def local(wavefunction, right_env, left_env, site_ops, right_map, left_map):
        K = right_env.shape[0]
        a, D, Q, N, _ = wavefunction.shape
        T = O * U
        small = T * K * D * N * N * 2 <= (8 << 20)
        if small and a == 1 and D == Z and D == T and N % (16 * T * PARTS) == 0 and N == 128:
            return fused_plan(Z, O, U, wavefunction, right_env, left_env, site_ops, right_map, left_map)
        return routed_plan(wavefunction, right_env, left_env, site_ops, right_map, left_map)

    in_specs = (
        P(("groups", "sector"), None, None, None, None),
        P(("groups", "op", "sub"), "sector", None, None),
        P(("groups", "op", "sub"), "sector", None, None),
        P(("groups", "op", "sub"), None, None),
        P(("groups", "op", "sub"), None),
        P(("groups", "op", "sub"), None),
    )
    out_specs = P(("groups", "op", "sub"), "sector", None, None, None)
    return jax.shard_map(local, mesh=mesh, in_specs=in_specs, out_specs=out_specs, check_vma=False)
```

```python
import functools

import jax
import jax.numpy as jnp
from jax import lax
from jax.experimental import pallas as pl
from jax.experimental.pallas import tpu as pltpu
from jax.sharding import PartitionSpec as P

MESH = pl.DeviceIdType.MESH
BF16 = jnp.bfloat16
F32 = jnp.float32
PARTS = 1


def routed_plan(wavefunction, right_env, left_env, site_ops, right_map, left_map):
    highest = lax.Precision.HIGHEST
    term_count = right_env.shape[0]
    sectors = wavefunction.shape[1]
    sector_ids = jnp.arange(sectors, dtype=jnp.int32)
    right_full = lax.all_gather(right_env, "sector", axis=1, tiled=True)
    coupled_terms = []
    for term_index in range(term_count):
        images = jnp.einsum(
            "abpij,bjl->bapil",
            wavefunction,
            right_full[term_index],
            preferred_element_type=jnp.float32,
        )
        select = (right_map[term_index][:, None] == sector_ids[None, :]).astype(jnp.float32)
        routed = jnp.einsum("bc,bapil->acpil", select, images, precision=highest)
        coupled = jnp.einsum(
            "pq,acpil->acqil", site_ops[term_index], routed, precision=highest
        ).astype(jnp.bfloat16)
        coupled_terms.append(coupled)
    coupled_all = jnp.stack(coupled_terms, axis=0)
    source_select = (left_map[:, :, None] == sector_ids[None, None, :]).astype(jnp.bfloat16)
    local_products = jnp.einsum(
        "taim,tacqil->tacqml", left_env, coupled_all, preferred_element_type=jnp.float32
    ).astype(jnp.bfloat16)
    term_partial = jnp.einsum(
        "tad,tacqml->dcqml",
        source_select,
        lax.all_to_all(local_products, "sector", split_axis=2, concat_axis=1, tiled=True),
        preferred_element_type=jnp.float32,
    )
    reduced = lax.psum_scatter(term_partial, ("op", "sub"), scatter_dimension=0, tiled=True)
    return reduced.astype(jnp.bfloat16)


def fused_kernel(Z, O, U, K, D, Q, N, H, order, psi_hbm, r_hbm, l_hbm, s_hbm, rm_hbm, lm_hbm, out_ref, psi_ref, r_ref, l_ref, s_ref, rm_ref, lm_ref, tab_ref, stage, rbuf, lbuf, tabs, lm, mask, cp, pf, psend, prcv, fin,
                 in_sem, t_send, t_recv, up_send, dn_send, l_send, l_recv, tab_send, tab_recv, p_send, p_recv, f_send, f_recv):
    T = O * U
    W = N // T
    LH = W // H
    z = lax.axis_index("sector")
    o = lax.axis_index("op")
    u = lax.axis_index("sub")
    t = o * U + u
    peers = []
    for i in range(O):
        for j in range(U):
            if i or j:
                po, pu = lax.rem(o + i, O), lax.rem(u + j, U)
                peers.append((i * U + j, po * U + pu, {"op": po, "sub": pu}))
    zpeers = [(r, lax.rem(z + r, Z)) for r in range(1, Z)]

    r_in = pltpu.make_async_copy(r_hbm, r_ref, in_sem.at[0])
    l_in = pltpu.make_async_copy(l_hbm, l_ref, in_sem.at[1])
    psi_in = pltpu.make_async_copy(psi_hbm, psi_ref, in_sem.at[2])
    s_in = pltpu.make_async_copy(s_hbm, s_ref, in_sem.at[3])
    rm_in = pltpu.make_async_copy(rm_hbm, rm_ref, in_sem.at[4])
    lm_in = pltpu.make_async_copy(lm_hbm, lm_ref, in_sem.at[5])
    for copy in (r_in, s_in, rm_in, lm_in, l_in, psi_in):
        copy.start()

    barrier = pltpu.get_barrier_semaphore()
    for e, pt, dev in peers:
        pl.semaphore_signal(barrier, inc=1, device_id=dev, device_id_type=MESH)
    for r, pz in zpeers:
        pl.semaphore_signal(barrier, inc=1, device_id={"sector": pz}, device_id_type=MESH)

    r_in.wait()
    for k in range(K):
        turned = r_ref[k, 0].astype(F32).T.astype(BF16)
        for tt in range(T):
            for h in range(H):
                at = tt * W + h * LH
                stage[tt, h, k] = turned[at:at + LH]
    for h in range(H):
        rbuf[z, h, 0] = stage[t, h]

    for copy in (s_in, rm_in, lm_in):
        copy.wait()
    tab_ref[...] = jnp.zeros_like(tab_ref)
    tab_ref[0:K, 0:D] = rm_ref[...].astype(F32)
    moved = lm_ref[...].astype(F32)
    column = lax.broadcasted_iota(jnp.int32, (K, D), 1)
    tab_ref[0:K, D:D + 1] = jnp.sum(jnp.where(column == z, moved, 0.0), axis=1, keepdims=True)
    for p in range(Q):
        tab_ref[8 + p * Q:8 + (p + 1) * Q, 0:K] = s_ref[p]

    pl.semaphore_wait(barrier, len(peers) + len(zpeers))

    def rcopy(e, pt, dev, h):
        return pltpu.make_async_remote_copy(
            src_ref=stage.at[pt, h], dst_ref=rbuf.at[z, h, e],
            send_sem=t_send.at[h, e], recv_sem=t_recv.at[z, h, e], device_id=dev, device_id_type=MESH)

    def tcopy(e, pt, dev):
        return pltpu.make_async_remote_copy(
            src_ref=tab_ref, dst_ref=tabs.at[e - 1],
            send_sem=tab_send.at[e - 1], recv_sem=tab_recv.at[e - 1], device_id=dev, device_id_type=MESH)

    def lcopy(e, pt, dev):
        return pltpu.make_async_remote_copy(
            src_ref=l_ref, dst_ref=lbuf.at[e - 1],
            send_sem=l_send.at[e - 1], recv_sem=l_recv.at[e - 1], device_id=dev, device_id_type=MESH)

    def lrelay(e):
        return pltpu.make_async_remote_copy(
            src_ref=lbuf.at[e - e % U - 1], dst_ref=lbuf.at[e - 1], send_sem=l_send.at[e - 1], recv_sem=l_recv.at[e - 1],
            device_id={"op": o, "sub": lax.rem(u + e % U, U)}, device_id_type=MESH)

    relayed = [e for e in range(U, T) if e % U]

    def up(b, h, e):
        return pltpu.make_async_remote_copy(
            src_ref=rbuf.at[b, h, e], dst_ref=rbuf.at[b, h, e],
            send_sem=up_send.at[b, h, e], recv_sem=t_recv.at[b, h, e], device_id={"sector": z + 1}, device_id_type=MESH)

    def down(b, h, e):
        return pltpu.make_async_remote_copy(
            src_ref=rbuf.at[b, h, e], dst_ref=rbuf.at[b, h, e],
            send_sem=dn_send.at[b, h, e], recv_sem=t_recv.at[b, h, e], device_id={"sector": z - 1}, device_id_type=MESH)

    def pcopy(h, r, pz):
        return pltpu.make_async_remote_copy(
            src_ref=psend.at[h, pz], dst_ref=prcv.at[h, z],
            send_sem=p_send.at[h, r - 1], recv_sem=p_recv.at[h, z], device_id={"sector": pz}, device_id_type=MESH)

    def fcopy(h, e, pt, dev):
        return pltpu.make_async_remote_copy(
            src_ref=fin.at[h, pt], dst_ref=out_ref.at[t, h],
            send_sem=f_send.at[h, e - 1], recv_sem=f_recv.at[h, e - 1], device_id=dev, device_id_type=MESH)

    for h in range(H):
        for e, pt, dev in peers:
            rcopy(e, pt, dev, h).start()
        if h == 0:
            for e, pt, dev in peers:
                tcopy(e, pt, dev).start()
    l_in.wait()
    for e, pt, dev in peers:
        if e < U or e % U == 0:
            lcopy(e, pt, dev).start()

    def gather(h, r):
        if r == 0:
            for e in range(T):
                if e:
                    up(z, h, e).wait_recv()

                @pl.when(z < Z - 1)
                def _():
                    up(z, h, e).start()

                @pl.when(z > 0)
                def _():
                    down(z, h, e).start()
            return
        for e in range(T):
            @pl.when(z - r >= 0)
            def _():
                up(z - r, h, e).wait_recv()

                @pl.when(z < Z - 1)
                def _():
                    up(z - r, h, e).start()

            @pl.when(z + r <= Z - 1)
            def _():
                down(z + r, h, e).wait_recv()

                @pl.when(z > 0)
                def _():
                    down(z + r, h, e).start()

    def table(e):
        return tab_ref[...] if e == 0 else tabs[e - 1]

    def row(tab, at):
        return jnp.broadcast_to(tab[:, at:at + 1], (tab.shape[0], N))

    def prepare():
        psi_in.wait()
        for e, pt, dev in peers:
            tcopy(e, pt, dev).wait_recv()
        for e in range(T):
            tab = table(e)
            for b in range(D):
                want = row(tab, b)
                for c in range(D):
                    hit = jnp.where(want == float(c), 1.0, 0.0)
                    for k in range(K):
                        mask[c, (e * K + k) * LH:(e * K + k + 1) * LH, b * N:(b + 1) * N] = jnp.broadcast_to(hit[k:k + 1], (LH, N)).astype(BF16)

    def relay_left():
        for e in range(U, T, U):
            lcopy(e, peers[e - 1][1], peers[e - 1][2]).wait_recv()
            for f in range(e + 1, e + U):
                lrelay(f).start()

    def prepare_left():
        for e in range(1, U):
            lcopy(e, peers[e - 1][1], peers[e - 1][2]).wait_recv()
        for e in relayed:
            lrelay(e).wait_recv()
        for e in range(T):
            want = row(table(e), D)
            for d in range(D):
                hit = jnp.where(want == float(d), 1.0, 0.0)
                for k in range(K):
                    block = l_ref[k, 0] if e == 0 else lbuf[e - 1, k, 0]
                    lm[(e * K + k) * N:(e * K + k + 1) * N, d * N:(d + 1) * N] = block * jnp.broadcast_to(hit[k:k + 1], (N, N)).astype(BF16)

    def compute(h):
        rows = T * K * LH
        right = jnp.concatenate([rbuf[b, h].reshape(rows, N) for b in range(D)], axis=1)
        for c in range(D):
            masked = right * mask[c]
            routed = None
            for b in range(D):
                part = lax.dot_general(masked[:, b * N:(b + 1) * N], psi_ref[0, b].reshape(Q * N, N),
                                       (((1,), (1,)), ((), ())), preferred_element_type=F32)
                routed = part if routed is None else routed + part
            for e in range(T):
                tab = table(e)
                for k in range(K):
                    at = (e * K + k) * LH
                    for q in range(Q):
                        coupled = None
                        for p in range(Q):
                            weight = jnp.broadcast_to(tab[8 + p * Q + q:9 + p * Q + q, k:k + 1], (1, N))
                            part = routed[at:at + LH, p * N:(p + 1) * N] * weight
                            coupled = part if coupled is None else coupled + part
                        cp[(c * Q + q) * LH:(c * Q + q + 1) * LH, (e * K + k) * N:(e * K + k + 1) * N] = coupled.astype(BF16)

    def products(h):
        sums = jnp.dot(cp[...], lm[...], preferred_element_type=F32)
        for c in range(D):
            part = sums[c * Q * LH:(c + 1) * Q * LH]
            pf[h, c] = part
            psend[h, c] = part.astype(BF16)
        for r, pz in zpeers[::-1]:
            pcopy(h, r, pz).start()

    def finish(h):
        total = pf[h, z]
        for r, pz in zpeers:
            pltpu.make_async_remote_copy(
                src_ref=psend.at[h, pz], dst_ref=prcv.at[h, pz], send_sem=p_send.at[h, r - 1],
                recv_sem=p_recv.at[h, pz], device_id={"sector": pz}, device_id_type=MESH).wait_recv()
            total = total + prcv[h, pz].astype(F32)
        total = total.astype(BF16)
        for d in range(D):
            fin[h, d] = total[:, d * N:(d + 1) * N].reshape(Q, LH, N)
        for e, pt, dev in peers:
            fcopy(h, e, pt, dev).start()
        out_ref[t, h] = fin[h, t]

    for step in order:
        kind = step[0]
        if kind == "gather":
            gather(step[1], step[2])
        elif kind == "prepare":
            prepare()
        elif kind == "relay":
            relay_left()
        elif kind == "left":
            prepare_left()
        elif kind == "compute":
            compute(step[1])
        elif kind == "products":
            products(step[1])
        else:
            finish(step[1])

    for h in range(H):
        for e, pt, dev in peers:
            fcopy(h, e, pt, dev).wait_recv()
            fcopy(h, e, pt, dev).wait_send()
            rcopy(e, pt, dev, h).wait_send()
        for r, pz in zpeers:
            pcopy(h, r, pz).wait_send()
        for e in range(T):
            for r in range(Z):
                @pl.when(jnp.logical_and(z - r >= 0, z < Z - 1))
                def _():
                    up(z - r, h, e).wait_send()

                @pl.when(jnp.logical_and(z + r <= Z - 1, z > 0))
                def _():
                    down(z + r, h, e).wait_send()
    for e, pt, dev in peers:
        tcopy(e, pt, dev).wait_send()
        if e in relayed:
            lrelay(e).wait_send()
        else:
            lcopy(e, pt, dev).wait_send()


def steps(Z, H):
    if H == 1:
        order = [("gather", 0, 0), ("prepare",)]
        order += [("gather", 0, 1), ("relay",)]
        order += [("gather", 0, r) for r in range(2, Z - 1)]
        order += [("left",), ("gather", 0, Z - 1), ("compute", 0), ("products", 0), ("finish", 0)]
        return order
    order = [("gather", 0, 0), ("prepare",), ("gather", 0, 1), ("relay",), ("gather", 0, 2), ("gather", 1, 0), ("left",)]
    order += [("gather", 0, 3), ("gather", 1, 1), ("compute", 0), ("products", 0), ("gather", 1, 2)]
    order += [("gather", 1, 3), ("compute", 1), ("products", 1), ("finish", 0), ("finish", 1)]
    return order


def fused_plan(Z, O, U, wavefunction, right_env, left_env, site_ops, right_map, left_map):
    K = right_env.shape[0]
    _, D, Q, N, _ = wavefunction.shape
    T, H = O * U, PARTS
    LH = N // T // H
    tab = jax.ShapeDtypeStruct((8 + -(-Q * Q // 8) * 8, 128), F32)
    site = site_ops.transpose(1, 2, 0)
    dma = pltpu.SemaphoreType.DMA
    vmem = pl.BlockSpec(memory_space=pltpu.VMEM)
    hbm = pl.BlockSpec(memory_space=pltpu.HBM)
    out = pl.pallas_call(
        functools.partial(fused_kernel, Z, O, U, K, D, Q, N, H, steps(Z, H)),
        out_shape=jax.ShapeDtypeStruct((T, H, Q, LH, N), BF16),
        in_specs=[hbm] * 6,
        out_specs=vmem,
        scratch_shapes=[
            pltpu.VMEM(wavefunction.shape, BF16),
            pltpu.VMEM(right_env.shape, BF16),
            pltpu.VMEM(left_env.shape, BF16),
            pltpu.VMEM(site.shape, F32),
            pltpu.VMEM(right_map.shape, jnp.int32),
            pltpu.VMEM(left_map.shape, jnp.int32),
            pltpu.VMEM(tab.shape, F32),
            pltpu.VMEM((T, H, K, LH, N), BF16),
            pltpu.VMEM((D, H, T, K, LH, N), BF16),
            pltpu.VMEM((T - 1,) + left_env.shape, BF16),
            pltpu.VMEM((T - 1,) + tab.shape, F32),
            pltpu.VMEM((T * K * N, D * N), BF16),
            pltpu.VMEM((D, T * K * LH, D * N), BF16),
            pltpu.VMEM((D * Q * LH, T * K * N), BF16),
            pltpu.VMEM((H, D, Q * LH, D * N), F32),
            pltpu.VMEM((H, D, Q * LH, D * N), BF16),
            pltpu.VMEM((H, D, Q * LH, D * N), BF16),
            pltpu.VMEM((H, D, Q, LH, N), BF16),
            dma((6,)), dma((H, T)), dma((D, H, T)), dma((D, H, T)), dma((D, H, T)),
            dma((T - 1,)), dma((T - 1,)), dma((T - 1,)), dma((T - 1,)),
            dma((H, Z - 1)), dma((H, Z)), dma((H, T - 1)), dma((H, T - 1)),
        ],
        compiler_params=pltpu.CompilerParams(collective_id=0, has_side_effects=True, vmem_limit_bytes=60 << 20),
        name="sigma",
    )(wavefunction, right_env, left_env, site, right_map, left_map)
    out = out.transpose(2, 4, 0, 1, 3).reshape(1, 1, Q, N, N)
    return out


def solution(mesh):
    shape = mesh.shape
    Z, O, U = shape["sector"], shape["op"], shape["sub"]

    def local(wavefunction, right_env, left_env, site_ops, right_map, left_map):
        K = right_env.shape[0]
        a, D, Q, N, _ = wavefunction.shape
        T = O * U
        small = T * K * D * N * N * 2 <= (8 << 20)
        if small and a == 1 and D == Z and D == T and Z > 2 and K <= 8 and N % (16 * T * PARTS) == 0 and N == 128:
            return fused_plan(Z, O, U, wavefunction, right_env, left_env, site_ops, right_map, left_map)
        return routed_plan(wavefunction, right_env, left_env, site_ops, right_map, left_map)

    in_specs = (
        P(("groups", "sector"), None, None, None, None),
        P(("groups", "op", "sub"), "sector", None, None),
        P(("groups", "op", "sub"), "sector", None, None),
        P(("groups", "op", "sub"), None, None),
        P(("groups", "op", "sub"), None),
        P(("groups", "op", "sub"), None),
    )
    out_specs = P(("groups", "op", "sub"), "sector", None, None, None)
    return jax.shard_map(local, mesh=mesh, in_specs=in_specs, out_specs=out_specs, check_vma=False)
```

```python
import functools

import jax
import jax.numpy as jnp
from jax import lax
from jax.experimental import pallas as pl
from jax.experimental.pallas import tpu as pltpu
from jax.sharding import PartitionSpec as P

MESH = pl.DeviceIdType.MESH
BF16 = jnp.bfloat16
F32 = jnp.float32
PARTS = 1


def routed_plan(wavefunction, right_env, left_env, site_ops, right_map, left_map):
    highest = lax.Precision.HIGHEST
    term_count = right_env.shape[0]
    sectors = wavefunction.shape[1]
    sector_ids = jnp.arange(sectors, dtype=jnp.int32)
    right_full = lax.all_gather(right_env, "sector", axis=1, tiled=True)
    coupled_terms = []
    for term_index in range(term_count):
        images = jnp.einsum(
            "abpij,bjl->bapil",
            wavefunction,
            right_full[term_index],
            preferred_element_type=jnp.float32,
        )
        select = (right_map[term_index][:, None] == sector_ids[None, :]).astype(jnp.float32)
        routed = jnp.einsum("bc,bapil->acpil", select, images, precision=highest)
        coupled = jnp.einsum(
            "pq,acpil->acqil", site_ops[term_index], routed, precision=highest
        ).astype(jnp.bfloat16)
        coupled_terms.append(coupled)
    coupled_all = jnp.stack(coupled_terms, axis=0)
    source_select = (left_map[:, :, None] == sector_ids[None, None, :]).astype(jnp.bfloat16)
    local_products = jnp.einsum(
        "taim,tacqil->tacqml", left_env, coupled_all, preferred_element_type=jnp.float32
    ).astype(jnp.bfloat16)
    term_partial = jnp.einsum(
        "tad,tacqml->dcqml",
        source_select,
        lax.all_to_all(local_products, "sector", split_axis=2, concat_axis=1, tiled=True),
        preferred_element_type=jnp.float32,
    )
    reduced = lax.psum_scatter(term_partial, ("op", "sub"), scatter_dimension=0, tiled=True)
    return reduced.astype(jnp.bfloat16)


def fused_kernel(Z, O, U, K, D, Q, N, H, order, psi_hbm, r_hbm, l_hbm, s_hbm, rm_hbm, lm_hbm, out_ref, psi_ref, r_ref, l_ref, s_ref, rm_ref, lm_ref, tab_ref, stage, rbuf, lbuf, tabs, lm, mask, cp, pf, psend, prcv, fin,
                 in_sem, t_send, t_recv, up_send, dn_send, l_send, l_recv, tab_send, tab_recv, p_send, p_recv, f_send, f_recv):
    T = O * U
    W = N // T
    LH = W // H
    z = lax.axis_index("sector")
    o = lax.axis_index("op")
    u = lax.axis_index("sub")
    t = o * U + u
    peers = []
    for i in range(O):
        for j in range(U):
            if i or j:
                po, pu = lax.rem(o + i, O), lax.rem(u + j, U)
                peers.append((i * U + j, po * U + pu, {"op": po, "sub": pu}))
    zpeers = [(r, lax.rem(z + r, Z)) for r in range(1, Z)]

    r_in = pltpu.make_async_copy(r_hbm, r_ref, in_sem.at[0])
    l_in = pltpu.make_async_copy(l_hbm, l_ref, in_sem.at[1])
    psi_in = pltpu.make_async_copy(psi_hbm, psi_ref, in_sem.at[2])
    s_in = pltpu.make_async_copy(s_hbm, s_ref, in_sem.at[3])
    rm_in = pltpu.make_async_copy(rm_hbm, rm_ref, in_sem.at[4])
    lm_in = pltpu.make_async_copy(lm_hbm, lm_ref, in_sem.at[5])
    for copy in (r_in, s_in, rm_in, lm_in, l_in, psi_in):
        copy.start()

    barrier = pltpu.get_barrier_semaphore()
    for e, pt, dev in peers:
        pl.semaphore_signal(barrier, inc=1, device_id=dev, device_id_type=MESH)
    for near, there in ((z + 1, z < Z - 1), (z - 1, z > 0)):
        @pl.when(there)
        def _():
            pl.semaphore_signal(barrier, inc=1, device_id={"sector": near}, device_id_type=MESH)

    r_in.wait()
    for k in range(K):
        turned = r_ref[k, 0].astype(F32).T.astype(BF16)
        for tt in range(T):
            for h in range(H):
                at = tt * W + h * LH
                stage[tt, h, k] = turned[at:at + LH]
    for h in range(H):
        rbuf[z, h, 0] = stage[t, h]

    for copy in (s_in, rm_in, lm_in):
        copy.wait()
    tab_ref[...] = jnp.zeros_like(tab_ref)
    tab_ref[0:K, 0:D] = rm_ref[...].astype(F32)
    moved = lm_ref[...].astype(F32)
    column = lax.broadcasted_iota(jnp.int32, (K, D), 1)
    tab_ref[0:K, D:D + 1] = jnp.sum(jnp.where(column == z, moved, 0.0), axis=1, keepdims=True)
    for p in range(Q):
        tab_ref[8 + p * Q:8 + (p + 1) * Q, 0:K] = s_ref[p]

    pl.semaphore_wait(barrier, len(peers) + jnp.where(z < Z - 1, 1, 0) + jnp.where(z > 0, 1, 0))

    def rcopy(e, pt, dev, h):
        return pltpu.make_async_remote_copy(
            src_ref=stage.at[pt, h], dst_ref=rbuf.at[z, h, e],
            send_sem=t_send.at[h, e], recv_sem=t_recv.at[z, h, e], device_id=dev, device_id_type=MESH)

    def tcopy(e, pt, dev):
        return pltpu.make_async_remote_copy(
            src_ref=tab_ref, dst_ref=tabs.at[e - 1],
            send_sem=tab_send.at[e - 1], recv_sem=tab_recv.at[e - 1], device_id=dev, device_id_type=MESH)

    def lcopy(e, pt, dev):
        return pltpu.make_async_remote_copy(
            src_ref=l_ref, dst_ref=lbuf.at[e - 1],
            send_sem=l_send.at[e - 1], recv_sem=l_recv.at[e - 1], device_id=dev, device_id_type=MESH)

    def lrelay(e):
        return pltpu.make_async_remote_copy(
            src_ref=lbuf.at[e - e % U - 1], dst_ref=lbuf.at[e - 1], send_sem=l_send.at[e - 1], recv_sem=l_recv.at[e - 1],
            device_id={"op": o, "sub": lax.rem(u + e % U, U)}, device_id_type=MESH)

    relayed = [e for e in range(U, T) if e % U]

    def up(b, h, e):
        return pltpu.make_async_remote_copy(
            src_ref=rbuf.at[b, h, e], dst_ref=rbuf.at[b, h, e],
            send_sem=up_send.at[b, h, e], recv_sem=t_recv.at[b, h, e], device_id={"sector": z + 1}, device_id_type=MESH)

    def down(b, h, e):
        return pltpu.make_async_remote_copy(
            src_ref=rbuf.at[b, h, e], dst_ref=rbuf.at[b, h, e],
            send_sem=dn_send.at[b, h, e], recv_sem=t_recv.at[b, h, e], device_id={"sector": z - 1}, device_id_type=MESH)

    def pcopy(h, r, pz):
        return pltpu.make_async_remote_copy(
            src_ref=psend.at[h, pz], dst_ref=prcv.at[h, z],
            send_sem=p_send.at[h, r - 1], recv_sem=p_recv.at[h, z], device_id={"sector": pz}, device_id_type=MESH)

    def fcopy(h, e, pt, dev):
        return pltpu.make_async_remote_copy(
            src_ref=fin.at[h, pt], dst_ref=out_ref.at[:, t, h],
            send_sem=f_send.at[h, e - 1], recv_sem=f_recv.at[h, e - 1], device_id=dev, device_id_type=MESH)

    for h in range(H):
        for e, pt, dev in peers:
            rcopy(e, pt, dev, h).start()
        if h == 0:
            for e, pt, dev in peers:
                tcopy(e, pt, dev).start()

    def gather(h, r):
        if r == 0:
            for e in range(T):
                if e:
                    up(z, h, e).wait_recv()

                @pl.when(z < Z - 1)
                def _():
                    up(z, h, e).start()

                @pl.when(z > 0)
                def _():
                    down(z, h, e).start()
            return
        for e in range(T):
            @pl.when(z - r >= 0)
            def _():
                up(z - r, h, e).wait_recv()

                @pl.when(z < Z - 1)
                def _():
                    up(z - r, h, e).start()

            @pl.when(z + r <= Z - 1)
            def _():
                down(z + r, h, e).wait_recv()

                @pl.when(z > 0)
                def _():
                    down(z + r, h, e).start()

    def table(e):
        return tab_ref[...] if e == 0 else tabs[e - 1]

    def row(tab, at):
        return jnp.broadcast_to(tab[:, at:at + 1], (tab.shape[0], N))

    def prepare():
        psi_in.wait()
        for e, pt, dev in peers:
            tcopy(e, pt, dev).wait_recv()
        for e in range(T):
            tab = table(e)
            for b in range(D):
                want = row(tab, b)
                for c in range(D):
                    hit = jnp.where(want == float(c), 1.0, 0.0)
                    for k in range(K):
                        mask[c, (e * K + k) * LH:(e * K + k + 1) * LH, b * N:(b + 1) * N] = jnp.broadcast_to(hit[k:k + 1], (LH, N)).astype(BF16)

    def send_left():
        l_in.wait()
        for e, pt, dev in peers:
            if e < U or e % U == 0:
                lcopy(e, pt, dev).start()

    def relay_left():
        for e in range(U, T, U):
            lcopy(e, peers[e - 1][1], peers[e - 1][2]).wait_recv()
            for f in range(e + 1, e + U):
                lrelay(f).start()

    def prepare_left():
        for e in range(1, U):
            lcopy(e, peers[e - 1][1], peers[e - 1][2]).wait_recv()
        for e in relayed:
            lrelay(e).wait_recv()
        for e in range(T):
            want = row(table(e), D)
            for d in range(D):
                hit = jnp.where(want == float(d), 1.0, 0.0)
                for k in range(K):
                    block = l_ref[k, 0] if e == 0 else lbuf[e - 1, k, 0]
                    lm[(e * K + k) * N:(e * K + k + 1) * N, d * N:(d + 1) * N] = block * jnp.broadcast_to(hit[k:k + 1], (N, N)).astype(BF16)

    def compute(h):
        rows = T * K * LH
        right = jnp.concatenate([rbuf[b, h].reshape(rows, N) for b in range(D)], axis=1)
        for c in range(D):
            masked = right * mask[c]
            routed = None
            for b in range(D):
                part = lax.dot_general(masked[:, b * N:(b + 1) * N], psi_ref[0, b].reshape(Q * N, N),
                                       (((1,), (1,)), ((), ())), preferred_element_type=F32)
                routed = part if routed is None else routed + part
            for e in range(T):
                tab = table(e)
                for k in range(K):
                    at = (e * K + k) * LH
                    for q in range(Q):
                        coupled = None
                        for p in range(Q):
                            weight = jnp.broadcast_to(tab[8 + p * Q + q:9 + p * Q + q, k:k + 1], (1, N))
                            part = routed[at:at + LH, p * N:(p + 1) * N] * weight
                            coupled = part if coupled is None else coupled + part
                        cp[(c * Q + q) * LH:(c * Q + q + 1) * LH, (e * K + k) * N:(e * K + k + 1) * N] = coupled.astype(BF16)

    def products(h):
        sums = jnp.dot(cp[...], lm[...], preferred_element_type=F32)
        for c in range(D):
            part = sums[c * Q * LH:(c + 1) * Q * LH]
            pf[h, c] = part
            psend[h, c] = part.astype(BF16)
        for r, pz in zpeers[::-1]:
            pcopy(h, r, pz).start()

    def finish(h):
        total = pf[h, z]
        for r, pz in zpeers:
            pltpu.make_async_remote_copy(
                src_ref=psend.at[h, pz], dst_ref=prcv.at[h, pz], send_sem=p_send.at[h, r - 1],
                recv_sem=p_recv.at[h, pz], device_id={"sector": pz}, device_id_type=MESH).wait_recv()
            total = total + prcv[h, pz].astype(F32)
        total = total.astype(BF16)
        for d in range(D):
            fin[h, d] = total[:, d * N:(d + 1) * N].reshape(Q, LH, N)
        for e, pt, dev in peers:
            fcopy(h, e, pt, dev).start()
        out_ref[:, t, h] = fin[h, t]

    for step in order:
        kind = step[0]
        if kind == "gather":
            gather(step[1], step[2])
        elif kind == "prepare":
            prepare()
        elif kind == "send":
            send_left()
        elif kind == "relay":
            relay_left()
        elif kind == "left":
            prepare_left()
        elif kind == "compute":
            compute(step[1])
        elif kind == "products":
            products(step[1])
        else:
            finish(step[1])

    for h in range(H):
        for e, pt, dev in peers:
            fcopy(h, e, pt, dev).wait_recv()
            fcopy(h, e, pt, dev).wait_send()
            rcopy(e, pt, dev, h).wait_send()
        for r, pz in zpeers:
            pcopy(h, r, pz).wait_send()
        for e in range(T):
            for r in range(Z):
                @pl.when(jnp.logical_and(z - r >= 0, z < Z - 1))
                def _():
                    up(z - r, h, e).wait_send()

                @pl.when(jnp.logical_and(z + r <= Z - 1, z > 0))
                def _():
                    down(z + r, h, e).wait_send()
    for e, pt, dev in peers:
        tcopy(e, pt, dev).wait_send()
        if e in relayed:
            lrelay(e).wait_send()
        else:
            lcopy(e, pt, dev).wait_send()


def steps(Z, H):
    if H == 1:
        order = [("gather", 0, 0), ("send",), ("prepare",)]
        order += [("gather", 0, 1), ("relay",)]
        order += [("gather", 0, r) for r in range(2, Z - 1)]
        order += [("left",), ("gather", 0, Z - 1), ("compute", 0), ("products", 0), ("finish", 0)]
        return order
    order = [("gather", 0, 0), ("prepare",), ("gather", 0, 1), ("relay",), ("gather", 0, 2), ("gather", 1, 0), ("left",)]
    order += [("gather", 0, 3), ("gather", 1, 1), ("compute", 0), ("products", 0), ("gather", 1, 2)]
    order += [("gather", 1, 3), ("compute", 1), ("products", 1), ("finish", 0), ("finish", 1)]
    return order


def fused_plan(Z, O, U, wavefunction, right_env, left_env, site_ops, right_map, left_map):
    K = right_env.shape[0]
    _, D, Q, N, _ = wavefunction.shape
    T, H = O * U, PARTS
    LH = N // T // H
    tab = jax.ShapeDtypeStruct((8 + -(-Q * Q // 8) * 8, 128), F32)
    site = site_ops.transpose(1, 2, 0)
    dma = pltpu.SemaphoreType.DMA
    vmem = pl.BlockSpec(memory_space=pltpu.VMEM)
    hbm = pl.BlockSpec(memory_space=pltpu.HBM)
    out = pl.pallas_call(
        functools.partial(fused_kernel, Z, O, U, K, D, Q, N, H, steps(Z, H)),
        out_shape=jax.ShapeDtypeStruct((Q, T, H, LH, N), BF16),
        in_specs=[hbm] * 6,
        out_specs=vmem,
        scratch_shapes=[
            pltpu.VMEM(wavefunction.shape, BF16),
            pltpu.VMEM(right_env.shape, BF16),
            pltpu.VMEM(left_env.shape, BF16),
            pltpu.VMEM(site.shape, F32),
            pltpu.VMEM(right_map.shape, jnp.int32),
            pltpu.VMEM(left_map.shape, jnp.int32),
            pltpu.VMEM(tab.shape, F32),
            pltpu.VMEM((T, H, K, LH, N), BF16),
            pltpu.VMEM((D, H, T, K, LH, N), BF16),
            pltpu.VMEM((T - 1,) + left_env.shape, BF16),
            pltpu.VMEM((T - 1,) + tab.shape, F32),
            pltpu.VMEM((T * K * N, D * N), BF16),
            pltpu.VMEM((D, T * K * LH, D * N), BF16),
            pltpu.VMEM((D * Q * LH, T * K * N), BF16),
            pltpu.VMEM((H, D, Q * LH, D * N), F32),
            pltpu.VMEM((H, D, Q * LH, D * N), BF16),
            pltpu.VMEM((H, D, Q * LH, D * N), BF16),
            pltpu.VMEM((H, D, Q, LH, N), BF16),
            dma((6,)), dma((H, T)), dma((D, H, T)), dma((D, H, T)), dma((D, H, T)),
            dma((T - 1,)), dma((T - 1,)), dma((T - 1,)), dma((T - 1,)),
            dma((H, Z - 1)), dma((H, Z)), dma((H, T - 1)), dma((H, T - 1)),
        ],
        compiler_params=pltpu.CompilerParams(collective_id=0, has_side_effects=True, vmem_limit_bytes=60 << 20),
        name="sigma",
    )(wavefunction, right_env, left_env, site, right_map, left_map)
    return out.reshape(1, 1, Q, N, N).swapaxes(3, 4)


def solution(mesh):
    shape = mesh.shape
    Z, O, U = shape["sector"], shape["op"], shape["sub"]

    def local(wavefunction, right_env, left_env, site_ops, right_map, left_map):
        K = right_env.shape[0]
        a, D, Q, N, _ = wavefunction.shape
        T = O * U
        small = T * K * D * N * N * 2 <= (8 << 20)
        if small and a == 1 and D == Z and D == T and Z > 2 and K <= 8 and N % (16 * T * PARTS) == 0 and N == 128:
            return fused_plan(Z, O, U, wavefunction, right_env, left_env, site_ops, right_map, left_map)
        return routed_plan(wavefunction, right_env, left_env, site_ops, right_map, left_map)

    in_specs = (
        P(("groups", "sector"), None, None, None, None),
        P(("groups", "op", "sub"), "sector", None, None),
        P(("groups", "op", "sub"), "sector", None, None),
        P(("groups", "op", "sub"), None, None),
        P(("groups", "op", "sub"), None),
        P(("groups", "op", "sub"), None),
    )
    out_specs = P(("groups", "op", "sub"), "sector", None, None, None)
    return jax.shard_map(local, mesh=mesh, in_specs=in_specs, out_specs=out_specs, check_vma=False)
```

```python
import functools

import jax
import jax.numpy as jnp
from jax import lax
from jax.experimental import pallas as pl
from jax.experimental.pallas import tpu as pltpu
from jax.sharding import PartitionSpec as P

MESH = pl.DeviceIdType.MESH
BF16 = jnp.bfloat16
F32 = jnp.float32
PARTS = 1


def routed_plan(wavefunction, right_env, left_env, site_ops, right_map, left_map):
    highest = lax.Precision.HIGHEST
    term_count = right_env.shape[0]
    sectors = wavefunction.shape[1]
    sector_ids = jnp.arange(sectors, dtype=jnp.int32)
    right_full = lax.all_gather(right_env, "sector", axis=1, tiled=True)
    coupled_terms = []
    for term_index in range(term_count):
        images = jnp.einsum(
            "abpij,bjl->bapil",
            wavefunction,
            right_full[term_index],
            preferred_element_type=jnp.float32,
        )
        select = (right_map[term_index][:, None] == sector_ids[None, :]).astype(jnp.float32)
        routed = jnp.einsum("bc,bapil->acpil", select, images, precision=highest)
        coupled = jnp.einsum(
            "pq,acpil->acqil", site_ops[term_index], routed, precision=highest
        ).astype(jnp.bfloat16)
        coupled_terms.append(coupled)
    coupled_all = jnp.stack(coupled_terms, axis=0)
    source_select = (left_map[:, :, None] == sector_ids[None, None, :]).astype(jnp.bfloat16)
    local_products = jnp.einsum(
        "taim,tacqil->tacqml", left_env, coupled_all, preferred_element_type=jnp.float32
    ).astype(jnp.bfloat16)
    term_partial = jnp.einsum(
        "tad,tacqml->dcqml",
        source_select,
        lax.all_to_all(local_products, "sector", split_axis=2, concat_axis=1, tiled=True),
        preferred_element_type=jnp.float32,
    )
    reduced = lax.psum_scatter(term_partial, ("op", "sub"), scatter_dimension=0, tiled=True)
    return reduced.astype(jnp.bfloat16)


def fused_kernel(Z, O, U, K, D, Q, N, H, order, psi_hbm, r_hbm, l_hbm, s_hbm, rm_hbm, lm_hbm, out_ref, psi_ref, r_ref, l_ref, s_ref, rm_ref, lm_ref, tab_ref, stage, rbuf, lbuf, tabs, lm, mask, cp, pf, psend, prcv, fin,
                 in_sem, t_send, t_recv, up_send, dn_send, l_send, l_recv, tab_send, tab_recv, p_send, p_recv, f_send, f_recv):
    T = O * U
    W = N // T
    LH = W // H
    z = lax.axis_index("sector")
    o = lax.axis_index("op")
    u = lax.axis_index("sub")
    t = o * U + u
    peers = []
    for i in range(O):
        for j in range(U):
            if i or j:
                po, pu = lax.rem(o + i, O), lax.rem(u + j, U)
                peers.append((i * U + j, po * U + pu, {"op": po, "sub": pu}))
    zpeers = [(r, lax.rem(z + r, Z)) for r in range(1, Z)]

    r_in = pltpu.make_async_copy(r_hbm, r_ref, in_sem.at[0])
    l_in = pltpu.make_async_copy(l_hbm, l_ref, in_sem.at[1])
    psi_in = pltpu.make_async_copy(psi_hbm, psi_ref, in_sem.at[2])
    s_in = pltpu.make_async_copy(s_hbm, s_ref, in_sem.at[3])
    rm_in = pltpu.make_async_copy(rm_hbm, rm_ref, in_sem.at[4])
    lm_in = pltpu.make_async_copy(lm_hbm, lm_ref, in_sem.at[5])
    for copy in (r_in, s_in, rm_in, lm_in, l_in, psi_in):
        copy.start()

    barrier = pltpu.get_barrier_semaphore()
    for e, pt, dev in peers:
        pl.semaphore_signal(barrier, inc=1, device_id=dev, device_id_type=MESH)
    for near, there in ((z + 1, z < Z - 1), (z - 1, z > 0)):
        @pl.when(there)
        def _():
            pl.semaphore_signal(barrier, inc=1, device_id={"sector": near}, device_id_type=MESH)

    r_in.wait()
    for k in range(K):
        turned = r_ref[k, 0].astype(F32).T.astype(BF16)
        for tt in range(T):
            for h in range(H):
                at = tt * W + h * LH
                stage[tt, h, k] = turned[at:at + LH]
    for h in range(H):
        rbuf[z, h, 0] = stage[t, h]

    for copy in (s_in, rm_in, lm_in):
        copy.wait()
    tab_ref[...] = jnp.zeros_like(tab_ref)
    tab_ref[0:K, 0:D] = rm_ref[...].astype(F32)
    moved = lm_ref[...].astype(F32)
    column = lax.broadcasted_iota(jnp.int32, (K, D), 1)
    tab_ref[0:K, D:D + 1] = jnp.sum(jnp.where(column == z, moved, 0.0), axis=1, keepdims=True)
    for p in range(Q):
        tab_ref[8 + p * Q:8 + (p + 1) * Q, 0:K] = s_ref[p]

    pl.semaphore_wait(barrier, len(peers) + jnp.where(z < Z - 1, 1, 0) + jnp.where(z > 0, 1, 0))

    def rcopy(e, pt, dev, h):
        return pltpu.make_async_remote_copy(
            src_ref=stage.at[pt, h], dst_ref=rbuf.at[z, h, e],
            send_sem=t_send.at[h, e], recv_sem=t_recv.at[z, h, e], device_id=dev, device_id_type=MESH)

    def tcopy(e, pt, dev):
        return pltpu.make_async_remote_copy(
            src_ref=tab_ref, dst_ref=tabs.at[e - 1],
            send_sem=tab_send.at[e - 1], recv_sem=tab_recv.at[e - 1], device_id=dev, device_id_type=MESH)

    def lcopy(e, pt, dev):
        return pltpu.make_async_remote_copy(
            src_ref=l_ref, dst_ref=lbuf.at[e - 1],
            send_sem=l_send.at[e - 1], recv_sem=l_recv.at[e - 1], device_id=dev, device_id_type=MESH)

    def lrelay(e):
        return pltpu.make_async_remote_copy(
            src_ref=lbuf.at[e - e % U - 1], dst_ref=lbuf.at[e - 1], send_sem=l_send.at[e - 1], recv_sem=l_recv.at[e - 1],
            device_id={"op": o, "sub": lax.rem(u + e % U, U)}, device_id_type=MESH)

    relayed = [e for e in range(U, T) if e % U]

    def up(b, h, e):
        return pltpu.make_async_remote_copy(
            src_ref=rbuf.at[b, h, e], dst_ref=rbuf.at[b, h, e],
            send_sem=up_send.at[b, h, e], recv_sem=t_recv.at[b, h, e], device_id={"sector": z + 1}, device_id_type=MESH)

    def down(b, h, e):
        return pltpu.make_async_remote_copy(
            src_ref=rbuf.at[b, h, e], dst_ref=rbuf.at[b, h, e],
            send_sem=dn_send.at[b, h, e], recv_sem=t_recv.at[b, h, e], device_id={"sector": z - 1}, device_id_type=MESH)

    def pcopy(h, r, pz):
        return pltpu.make_async_remote_copy(
            src_ref=psend.at[h, pz], dst_ref=prcv.at[h, z],
            send_sem=p_send.at[h, r - 1], recv_sem=p_recv.at[h, z], device_id={"sector": pz}, device_id_type=MESH)

    def fcopy(h, e, pt, dev):
        return pltpu.make_async_remote_copy(
            src_ref=fin.at[h, pt], dst_ref=out_ref.at[:, t, h],
            send_sem=f_send.at[h, e - 1], recv_sem=f_recv.at[h, e - 1], device_id=dev, device_id_type=MESH)

    for h in range(H):
        for e, pt, dev in peers:
            rcopy(e, pt, dev, h).start()
        if h == 0:
            for e, pt, dev in peers:
                tcopy(e, pt, dev).start()

    def gather(h, r):
        if r == 0:
            for e in range(T):
                if e:
                    up(z, h, e).wait_recv()

                @pl.when(z < Z - 1)
                def _():
                    up(z, h, e).start()

                @pl.when(z > 0)
                def _():
                    down(z, h, e).start()
            return
        for e in range(T):
            @pl.when(z - r >= 0)
            def _():
                up(z - r, h, e).wait_recv()

                @pl.when(z < Z - 1)
                def _():
                    up(z - r, h, e).start()

            @pl.when(z + r <= Z - 1)
            def _():
                down(z + r, h, e).wait_recv()

                @pl.when(z > 0)
                def _():
                    down(z + r, h, e).start()

    def table(e):
        return tab_ref[...] if e == 0 else tabs[e - 1]

    def row(tab, at):
        return jnp.broadcast_to(tab[:, at:at + 1], (tab.shape[0], N))

    def prepare():
        psi_in.wait()
        for e, pt, dev in peers:
            tcopy(e, pt, dev).wait_recv()
        for e in range(T):
            tab = table(e)
            for b in range(D):
                want = row(tab, b)
                for c in range(D):
                    hit = jnp.where(want == float(c), 1.0, 0.0)
                    for k in range(K):
                        mask[c, (e * K + k) * LH:(e * K + k + 1) * LH, b * N:(b + 1) * N] = jnp.broadcast_to(hit[k:k + 1], (LH, N)).astype(BF16)

    def send_left():
        l_in.wait()
        for e, pt, dev in peers:
            if e < U or e % U == 0:
                lcopy(e, pt, dev).start()

    def relay_left():
        for e in range(U, T, U):
            lcopy(e, peers[e - 1][1], peers[e - 1][2]).wait_recv()
            for f in range(e + 1, e + U):
                lrelay(f).start()

    def prepare_left():
        for e in range(1, U):
            lcopy(e, peers[e - 1][1], peers[e - 1][2]).wait_recv()
        for e in relayed:
            lrelay(e).wait_recv()
        for e in range(T):
            want = row(table(e), D)
            for d in range(D):
                hit = jnp.where(want == float(d), 1.0, 0.0)
                for k in range(K):
                    block = l_ref[k, 0] if e == 0 else lbuf[e - 1, k, 0]
                    lm[(e * K + k) * N:(e * K + k + 1) * N, d * N:(d + 1) * N] = block * jnp.broadcast_to(hit[k:k + 1], (N, N)).astype(BF16)

    def compute(h):
        rows = T * K * LH
        right = jnp.concatenate([rbuf[b, h].reshape(rows, N) for b in range(D)], axis=1)
        for c in range(D):
            masked = right * mask[c]
            routed = None
            for b in range(D):
                part = lax.dot_general(masked[:, b * N:(b + 1) * N], psi_ref[0, b].reshape(Q * N, N),
                                       (((1,), (1,)), ((), ())), preferred_element_type=F32)
                routed = part if routed is None else routed + part
            for e in range(T):
                tab = table(e)
                for k in range(K):
                    at = (e * K + k) * LH
                    for q in range(Q):
                        coupled = None
                        for p in range(Q):
                            weight = jnp.broadcast_to(tab[8 + p * Q + q:9 + p * Q + q, k:k + 1], (1, N))
                            part = routed[at:at + LH, p * N:(p + 1) * N] * weight
                            coupled = part if coupled is None else coupled + part
                        cp[(c * Q + q) * LH:(c * Q + q + 1) * LH, (e * K + k) * N:(e * K + k + 1) * N] = coupled.astype(BF16)

    def products(h):
        sums = jnp.dot(cp[...], lm[...], preferred_element_type=F32)
        for c in range(D):
            part = sums[c * Q * LH:(c + 1) * Q * LH]
            pf[h, c] = part
            psend[h, c] = part.astype(BF16)
        for r, pz in zpeers:
            pcopy(h, r, pz).start()

    def finish(h):
        total = pf[h, z]
        for r, pz in zpeers:
            pltpu.make_async_remote_copy(
                src_ref=psend.at[h, pz], dst_ref=prcv.at[h, pz], send_sem=p_send.at[h, r - 1],
                recv_sem=p_recv.at[h, pz], device_id={"sector": pz}, device_id_type=MESH).wait_recv()
            total = total + prcv[h, pz].astype(F32)
        total = total.astype(BF16)
        for d in range(D):
            fin[h, d] = total[:, d * N:(d + 1) * N].reshape(Q, LH, N)
        for e, pt, dev in peers:
            fcopy(h, e, pt, dev).start()
        out_ref[:, t, h] = fin[h, t]

    for step in order:
        kind = step[0]
        if kind == "gather":
            gather(step[1], step[2])
        elif kind == "prepare":
            prepare()
        elif kind == "send":
            send_left()
        elif kind == "relay":
            relay_left()
        elif kind == "left":
            prepare_left()
        elif kind == "compute":
            compute(step[1])
        elif kind == "products":
            products(step[1])
        else:
            finish(step[1])

    for h in range(H):
        for e, pt, dev in peers:
            fcopy(h, e, pt, dev).wait_recv()
            fcopy(h, e, pt, dev).wait_send()
            rcopy(e, pt, dev, h).wait_send()
        for r, pz in zpeers:
            pcopy(h, r, pz).wait_send()
        for e in range(T):
            for r in range(Z):
                @pl.when(jnp.logical_and(z - r >= 0, z < Z - 1))
                def _():
                    up(z - r, h, e).wait_send()

                @pl.when(jnp.logical_and(z + r <= Z - 1, z > 0))
                def _():
                    down(z + r, h, e).wait_send()
    for e, pt, dev in peers:
        tcopy(e, pt, dev).wait_send()
        if e in relayed:
            lrelay(e).wait_send()
        else:
            lcopy(e, pt, dev).wait_send()


def steps(Z, H):
    if H == 1:
        order = [("gather", 0, 0), ("send",), ("prepare",)]
        order += [("gather", 0, 1), ("relay",)]
        order += [("gather", 0, r) for r in range(2, Z - 1)]
        order += [("left",), ("gather", 0, Z - 1), ("compute", 0), ("products", 0), ("finish", 0)]
        return order
    order = [("gather", 0, 0), ("prepare",), ("gather", 0, 1), ("relay",), ("gather", 0, 2), ("gather", 1, 0), ("left",)]
    order += [("gather", 0, 3), ("gather", 1, 1), ("compute", 0), ("products", 0), ("gather", 1, 2)]
    order += [("gather", 1, 3), ("compute", 1), ("products", 1), ("finish", 0), ("finish", 1)]
    return order


def fused_plan(Z, O, U, wavefunction, right_env, left_env, site_ops, right_map, left_map):
    K = right_env.shape[0]
    _, D, Q, N, _ = wavefunction.shape
    T, H = O * U, PARTS
    LH = N // T // H
    tab = jax.ShapeDtypeStruct((8 + -(-Q * Q // 8) * 8, 128), F32)
    site = site_ops.transpose(1, 2, 0)
    dma = pltpu.SemaphoreType.DMA
    vmem = pl.BlockSpec(memory_space=pltpu.VMEM)
    hbm = pl.BlockSpec(memory_space=pltpu.HBM)
    out = pl.pallas_call(
        functools.partial(fused_kernel, Z, O, U, K, D, Q, N, H, steps(Z, H)),
        out_shape=jax.ShapeDtypeStruct((Q, T, H, LH, N), BF16),
        in_specs=[hbm] * 6,
        out_specs=vmem,
        scratch_shapes=[
            pltpu.VMEM(wavefunction.shape, BF16),
            pltpu.VMEM(right_env.shape, BF16),
            pltpu.VMEM(left_env.shape, BF16),
            pltpu.VMEM(site.shape, F32),
            pltpu.VMEM(right_map.shape, jnp.int32),
            pltpu.VMEM(left_map.shape, jnp.int32),
            pltpu.VMEM(tab.shape, F32),
            pltpu.VMEM((T, H, K, LH, N), BF16),
            pltpu.VMEM((D, H, T, K, LH, N), BF16),
            pltpu.VMEM((T - 1,) + left_env.shape, BF16),
            pltpu.VMEM((T - 1,) + tab.shape, F32),
            pltpu.VMEM((T * K * N, D * N), BF16),
            pltpu.VMEM((D, T * K * LH, D * N), BF16),
            pltpu.VMEM((D * Q * LH, T * K * N), BF16),
            pltpu.VMEM((H, D, Q * LH, D * N), F32),
            pltpu.VMEM((H, D, Q * LH, D * N), BF16),
            pltpu.VMEM((H, D, Q * LH, D * N), BF16),
            pltpu.VMEM((H, D, Q, LH, N), BF16),
            dma((6,)), dma((H, T)), dma((D, H, T)), dma((D, H, T)), dma((D, H, T)),
            dma((T - 1,)), dma((T - 1,)), dma((T - 1,)), dma((T - 1,)),
            dma((H, Z - 1)), dma((H, Z)), dma((H, T - 1)), dma((H, T - 1)),
        ],
        compiler_params=pltpu.CompilerParams(collective_id=0, has_side_effects=True, vmem_limit_bytes=60 << 20),
        name="sigma",
    )(wavefunction, right_env, left_env, site, right_map, left_map)
    return out.reshape(1, 1, Q, N, N).swapaxes(3, 4)


def solution(mesh):
    shape = mesh.shape
    Z, O, U = shape["sector"], shape["op"], shape["sub"]

    def local(wavefunction, right_env, left_env, site_ops, right_map, left_map):
        K = right_env.shape[0]
        a, D, Q, N, _ = wavefunction.shape
        T = O * U
        small = T * K * D * N * N * 2 <= (8 << 20)
        if small and a == 1 and D == Z and D == T and Z > 2 and K <= 8 and N % (16 * T * PARTS) == 0 and N == 128:
            return fused_plan(Z, O, U, wavefunction, right_env, left_env, site_ops, right_map, left_map)
        return routed_plan(wavefunction, right_env, left_env, site_ops, right_map, left_map)

    in_specs = (
        P(("groups", "sector"), None, None, None, None),
        P(("groups", "op", "sub"), "sector", None, None),
        P(("groups", "op", "sub"), "sector", None, None),
        P(("groups", "op", "sub"), None, None),
        P(("groups", "op", "sub"), None),
        P(("groups", "op", "sub"), None),
    )
    out_specs = P(("groups", "op", "sub"), "sector", None, None, None)
    return jax.shard_map(local, mesh=mesh, in_specs=in_specs, out_specs=out_specs, check_vma=False)
```
